32 devices in a mesh: dp: 16 (over z, y, core), tensor: 2 (over x).
Axes of the slice: x: 2, y: 2, z: 4, core: 2. Of those that a mesh axis runs over, the one named last changes fastest.
Arguments:
- tokens: bfloat16 [65536, 1024], P(('dp', 'tensor')), may hold values from -6 to 6
- cotangent: bfloat16 [65536, 1024], P(('dp', 'tensor')), may hold values from -6 to 6
- seq_lengths: int32 [32], replicated, may hold values from 1 to 2048, 40960 in all
- slot_seq: int32 [32], replicated, may hold values from 0 to 31, each once
- w_query: bfloat16 [1024, 1024], P('dp', 'tensor'), may hold values from -0.1875 to 0.1875
- w_key: bfloat16 [1024, 1024], P('dp', 'tensor'), may hold values from -0.1875 to 0.1875
- w_value: bfloat16 [1024, 1024], P('dp', 'tensor'), may hold values from -0.1875 to 0.1875
- b_query: bfloat16 [16, 64], P('tensor', 'dp'), may hold values from -1.5 to 1.5
- b_value: bfloat16 [16, 64], P('tensor', 'dp'), may hold values from -0.25 to 0.25
- w_output: bfloat16 [1024, 1024], P('tensor', 'dp'), may hold values from -2 to 2
- b_output: float32 [1024], P(('dp', 'tensor')), may hold values from -1.5 to 1.5
- gain_first: float32 [1024], P(('dp', 'tensor')), may hold values from 0.1 to 1.9
- shift_first: float32 [1024], P(('dp', 'tensor')), may hold values from -1.5 to 1.5
- w_up: bfloat16 [1024, 4096], P('dp', 'tensor'), may hold values from -0.1875 to 0.1875
- b_up: bfloat16 [64, 64], P('tensor', 'dp'), may hold values from -1.5 to 1.5
- w_down: bfloat16 [4096, 1024], P('tensor', 'dp'), may hold values from -0.09375 to 0.09375
- b_down: float32 [1024], P(('dp', 'tensor')), may hold values from -1.5 to 1.5
- gain_second: float32 [1024], P(('dp', 'tensor')), may hold values from 0.1 to 1.9
- shift_second: float32 [1024], P(('dp', 'tensor')), may hold values from -1.5 to 1.5
Outputs:
- layer_out: float32 [65536, 1024], P(('dp', 'tensor'))
- grad_tokens: float32 [65536, 1024], P(('dp', 'tensor'))
- grad_w_query: float32 [1024, 1024], P('dp', 'tensor')
- grad_w_key: float32 [1024, 1024], P('dp', 'tensor')
- grad_w_value: float32 [1024, 1024], P('dp', 'tensor')
- grad_b_query: float32 [16, 64], P('tensor', 'dp')
- grad_b_value: float32 [16, 64], P('tensor', 'dp')
- grad_w_output: float32 [1024, 1024], P('tensor', 'dp')
- grad_b_output: float32 [1024], P(('dp', 'tensor'))
- grad_gain_first: float32 [1024], P(('dp', 'tensor'))
- grad_shift_first: float32 [1024], P(('dp', 'tensor'))
- grad_w_up: float32 [1024, 4096], P('dp', 'tensor')
- grad_b_up: float32 [64, 64], P('tensor', 'dp')
- grad_w_down: float32 [4096, 1024], P('tensor', 'dp')
- grad_b_down: float32 [1024], P(('dp', 'tensor'))
- grad_gain_second: float32 [1024], P(('dp', 'tensor'))
- grad_shift_second: float32 [1024], P(('dp', 'tensor'))
The draws below stay inside these ranges and needn't reach their ends.
Inputs may be any that keep to these rules, and one draw needn't show every extreme that they name: `seq_lengths`: the lengths add up to 40960 and the longest is 2048. `slot_seq`: every sequence is in exactly one slot.
All inputs are finite; a program needn't handle non-finite values.
Results may differ from the reference program's by a relative error of at most 0.02.
Values may be sent and summed in bfloat16 or wider, within the bound.
A program may use at most 384 MiB of HBM per device.

```python
import math
import jax
import jax.numpy as jnp
import numpy as np
from jax import lax

D = 1024
HEADS = 16
HEAD_DIM = 64
FF = 4096
SEQ_MAX = 2048
SLOTS = 2
SEQS = 32
TOKENS = 65536
N_DP = 16


def with_spikes(entries, own_key, source, target, parts, factor):
    owner, partner = [(jnp.arange(entries.shape[dim]) // (entries.shape[dim] // parts)).reshape([-1 if axis == dim else 1 for axis in range(entries.ndim)]) for dim in (source, target)]
    chosen = jax.random.permutation(own_key, parts)[partner]
    strong = (owner == chosen) | (owner == (partner + parts // 2) % parts)
    return jnp.where(strong, factor * entries, entries)


def level_of(rng, extent, shards, low, high):
    level = 1.0
    for position, blocks in shards:
        heights = jax.random.uniform(jax.random.fold_in(jax.random.fold_in(rng, 6), position), (blocks,), jnp.float32, low / len(shards), high / len(shards))
        level = level * jnp.repeat(jnp.exp(heights), extent[position] // blocks).reshape((-1,) + (1,) * (len(extent) - 1 - position))
    return level


def length_profile(number_of, total, limit, slope):
    weights = [(1 << 20) // math.isqrt(rank ** slope) + 1 for rank in range(2, number_of + 1)]
    rest, counts = total - limit - (number_of - 1), [1] * (number_of - 1)
    while rest > 0:
        free = [i for i in range(number_of - 1) if counts[i] < limit]
        pool, remaining = sum([weights[i] for i in free]), rest
        for i in free:
            more = min(limit - counts[i], max(1, remaining * weights[i] // pool), rest)
            counts[i] = counts[i] + more
            rest = rest - more
    return np.array([limit] + counts)


def ragged_sizes(key, amount, total, most, lean):
    if amount == 2:
        one = jax.random.randint(key, (), max(1, total - most), min(most, total - 1) + 1)
        return jnp.stack([one, total - one])
    tallies = jnp.asarray(length_profile(amount, total, most, lean), jnp.int32)
    pairs = (amount - 1) // 2
    source_of, taker = tallies[1:1 + 2 * pairs:2], tallies[2:2 + 2 * pairs:2]
    slack = jnp.minimum(source_of - 1, most - taker)
    shifted = jax.random.randint(jax.random.fold_in(key, 1), (pairs,), 0, 1 << 20) % (slack + 1)
    tallies = tallies.at[1:1 + 2 * pairs:2].set(source_of - shifted).at[2:2 + 2 * pairs:2].set(taker + shifted)
    return tallies[jax.random.permutation(jax.random.fold_in(key, 2), amount)]


def scatter_about(stream_key, shape, spread, limit, cuts=(), kind=jnp.bfloat16):
    values = spread * jax.random.normal(stream_key, shape, jnp.float32)
    if cuts:
        values = values * level_of(stream_key, shape, cuts, -0.22, 0.18)
    return jnp.clip(values, -limit, limit).astype(kind)


def noise_with(key, dims, spread, limit, cuts, heavy, kind=jnp.bfloat16):
    values = spread * jax.random.normal(key, dims, jnp.float32)
    if cuts:
        values = values * level_of(key, dims, cuts, -0.22, 0.18)
    return jnp.clip(with_spikes(values, jax.random.fold_in(key, 3), *heavy), -limit, limit).astype(kind)


def setup_inputs(seed: int = 0) -> dict:
    key_list = jax.random.split(jax.random.key(seed), 20)
    tokens = scatter_about(key_list[0], (TOKENS, D), 1.0, 6.0, ((0, 32),))
    cotangent = noise_with(key_list[1], (TOKENS, D), 1.0, 6.0, ((0, 32),), (0, 1, 32, 2.75))
    seq_lengths = ragged_sizes(key_list[2], SEQS, SEQS * SEQ_MAX * 5 // 8, SEQ_MAX, 2).astype(jnp.int32)
    slot_seq = jax.random.permutation(key_list[3], SEQS).astype(jnp.int32)
    w_query = scatter_about(key_list[4], (D, D), D ** -0.5, 0.1875, ((0, 16), (1, 2)))
    w_key = scatter_about(key_list[5], (D, D), D ** -0.5, 0.1875, ((0, 16), (1, 2)))
    w_value = scatter_about(key_list[6], (D, D), D ** -0.5, 0.1875, ((0, 16), (1, 2)))
    b_query = scatter_about(key_list[7], (HEADS, HEAD_DIM), 0.3, 1.5, ((0, 2), (1, 16)))
    b_value = scatter_about(key_list[8], (HEADS, HEAD_DIM), 0.05, 0.25, ((0, 2), (1, 16)))
    w_output = scatter_about(key_list[9], (D, D), (max(D // 128, 1)) ** -0.5, 2.0, ((0, 2), (1, 16)))
    b_output = scatter_about(key_list[10], (D,), 0.3, 1.5, ((0, 32),), jnp.float32)
    gain_first = jnp.clip(1.0 + 0.18 * jax.random.normal(key_list[11], (D,), jnp.float32), 0.1, 1.9)
    shift_first = scatter_about(key_list[12], (D,), 0.3, 1.5, ((0, 32),), jnp.float32)
    w_up = scatter_about(key_list[13], (D, FF), D ** -0.5, 0.1875, ((0, 16), (1, 2)))
    b_up = scatter_about(key_list[14], (FF // HEAD_DIM, HEAD_DIM), 0.3, 1.5, ((0, 2), (1, 16)))
    w_down = scatter_about(key_list[15], (FF, D), FF ** -0.5, 0.09375, ((0, 2), (1, 16)))
    b_down = scatter_about(key_list[16], (D,), 0.3, 1.5, ((0, 32),), jnp.float32)
    gain_second = jnp.clip(1.0 + 0.18 * jax.random.normal(key_list[17], (D,), jnp.float32), 0.1, 1.9)
    shift_second = scatter_about(key_list[18], (D,), 0.3, 1.5, ((0, 32),), jnp.float32)
    return dict(tokens=tokens, cotangent=cotangent, seq_lengths=seq_lengths, slot_seq=slot_seq, w_query=w_query, w_key=w_key, w_value=w_value, b_query=b_query, b_value=b_value, w_output=w_output, b_output=b_output, gain_first=gain_first, shift_first=shift_first, w_up=w_up, b_up=b_up, w_down=w_down, b_down=b_down, gain_second=gain_second, shift_second=shift_second)


@jax.custom_vjp
def low(v):
    return lax.optimization_barrier(v.astype(jnp.bfloat16)).astype(jnp.float32)

@jax.custom_vjp
def low_back(v):
    return v

def low_keep(v):
    return (low(v), None)

def low_pass(kept, grad):
    return (grad,)

def back_keep(v):
    return (v, None)

def back_low(kept, grad):
    return (low(grad),)
low.defvjp(low_keep, low_pass)
low_back.defvjp(back_keep, back_low)
precise = lax.Precision.HIGHEST
norm_eps = 1e-06
masked_score = -1e+30

def layer_norm(resid, gain, shift):
    center = resid - lax.optimization_barrier(jnp.mean(resid, axis=-1, keepdims=True))
    variance = lax.optimization_barrier(jnp.mean(center * center, axis=-1, keepdims=True))
    return center * lax.rsqrt(variance + norm_eps) * gain + shift

def attend_slot(packed):
    queries, keys, values, length = packed
    scores = jnp.einsum('qhd,khd->hqk', queries, keys, precision=precise) * HEAD_DIM ** (-0.5)
    positions = jnp.arange(SEQ_MAX, dtype=jnp.int32)
    scores = jnp.where(positions[None, None, :] < length, scores, masked_score)
    scores = low_back(scores)
    row_peak = lax.optimization_barrier(jnp.max(scores, axis=-1, keepdims=True))
    exponent = jnp.exp(scores - row_peak)
    attn_probs = low(exponent / lax.optimization_barrier(jnp.sum(exponent, axis=-1, keepdims=True)))
    return jnp.einsum('hqk,khd->qhd', attn_probs, values, precision=precise)

def layer_rows(params, rows, lengths):
    w_query, w_key, w_value, b_query, b_value, w_output, b_output, gain_first, shift_first, w_up, b_up, w_down, b_down, gain_second, shift_second = params
    queries = low(low_back(jnp.dot(rows, w_query, precision=precise) + b_query.reshape(D)))
    keys = low(low_back(jnp.dot(rows, w_key, precision=precise)))
    values = low(low_back(jnp.dot(rows, w_value, precision=precise) + b_value.reshape(D)))
    shape_four = (SLOTS, SEQ_MAX, HEADS, HEAD_DIM)
    attended = lax.map(jax.checkpoint(attend_slot), (queries.reshape(shape_four), keys.reshape(shape_four), values.reshape(shape_four), lengths))
    mixed = low(low_back(attended.reshape(SLOTS * SEQ_MAX, D)))
    branch = low_back(jnp.dot(mixed, w_output, precision=precise) + b_output)
    normed = layer_norm(rows + branch, gain_first, shift_first)
    hidden_pre = low_back(jnp.dot(low(normed), w_up, precision=precise) + b_up.reshape(FF))
    hidden = low(jax.nn.gelu(hidden_pre, approximate=False))
    second = low_back(jnp.dot(hidden, w_down, precision=precise) + b_down)
    return layer_norm(normed + second, gain_second, shift_second)

def reference(tokens, cotangent, seq_lengths, slot_seq, w_query, w_key, w_value, b_query, b_value, w_output, b_output, gain_first, shift_first, w_up, b_up, w_down, b_down, gain_second, shift_second):
    params = tuple((weight.astype(jnp.float32) for weight in (w_query, w_key, w_value, b_query, b_value, w_output, b_output, gain_first, shift_first, w_up, b_up, w_down, b_down, gain_second, shift_second)))
    slot_len = seq_lengths[slot_seq].astype(jnp.int32).reshape(N_DP, SLOTS)
    group_rows = tokens.astype(jnp.float32).reshape(N_DP, SLOTS * SEQ_MAX, D)
    group_cot = cotangent.astype(jnp.float32).reshape(N_DP, SLOTS * SEQ_MAX, D)

    def one_group(running, pieces):
        rows, cot_rows, lengths = pieces
        outputs, pullback = jax.vjp(lambda weights, inputs: layer_rows(weights, inputs, lengths), params, rows)
        grad_params, grad_rows = pullback(cot_rows)
        running = jax.tree.map(lambda first_val, second_val: first_val + second_val, running, grad_params)
        return (running, (outputs, grad_rows))
    zeros_init = jax.tree.map(jnp.zeros_like, params)
    totals, (outputs, grads) = lax.scan(one_group, zeros_init, (group_rows, group_cot, slot_len))
    return (outputs.reshape(TOKENS, D), grads.reshape(TOKENS, D)) + tuple(totals)
```

```python
import jax
import jax.numpy as jnp
from jax import lax
from jax.experimental import pallas as pl
from jax.experimental.pallas import tpu as pltpu
from jax.sharding import PartitionSpec as P

HEAD_DIM = 64
SEQ_MAX = 2048


norm_eps = 1e-06
masked_score = -1e30


def matmul(left, right):
    return jnp.dot(left, right, preferred_element_type=jnp.float32)


def contract_rows(left, right):
    return lax.dot_general(
        left, right, (((0,), (0,)), ((), ())), preferred_element_type=jnp.float32
    )


def contract_cols(left, right):
    return lax.dot_general(
        left, right, (((1,), (1,)), ((), ())), preferred_element_type=jnp.float32
    )


def norm_forward(resid, gain, shift):
    center = resid - jnp.mean(resid, axis=-1, keepdims=True)
    inv_std = lax.rsqrt(jnp.mean(center * center, axis=-1, keepdims=True) + norm_eps)
    normal = center * inv_std
    return (normal * gain + shift, normal, inv_std)


def norm_backward(normal, inv_std, gain, upstream):
    scaled = upstream * gain
    mean_one = jnp.mean(scaled, axis=-1, keepdims=True)
    mean_two = jnp.mean(scaled * normal, axis=-1, keepdims=True)
    grad_resid = inv_std * (scaled - mean_one - normal * mean_two)
    return (grad_resid, jnp.sum(upstream * normal, axis=0), jnp.sum(upstream, axis=0))


def masked_scores(query_blk, keys_slot, length, scale):
    scores = (
        jnp.einsum("qhd,khd->hqk", query_blk, keys_slot, preferred_element_type=jnp.float32) * scale
    )
    positions = lax.broadcasted_iota(jnp.int32, scores.shape, 2)
    return jnp.where(positions < length, scores, masked_score)


def attention_forward(queries, keys, values, lengths, scale):
    rows_all = queries.shape[0]
    block_rows = min(512, SEQ_MAX)
    per_slot = SEQ_MAX // block_rows

    def attention_one_block(block_index):
        slot_index = block_index // per_slot
        query_blk = lax.dynamic_slice_in_dim(queries, block_index * block_rows, block_rows, 0)
        keys_slot = lax.dynamic_slice_in_dim(keys, slot_index * SEQ_MAX, SEQ_MAX, 0)
        values_slot = lax.dynamic_slice_in_dim(values, slot_index * SEQ_MAX, SEQ_MAX, 0)
        length = lax.dynamic_index_in_dim(lengths, slot_index, 0, keepdims=False)
        scores = masked_scores(query_blk, keys_slot, length, scale)
        row_peak = jnp.max(scores, axis=-1, keepdims=True)
        exponent = jnp.exp(scores - row_peak)
        summed = jnp.sum(exponent, axis=-1, keepdims=True)
        attn_probs = (exponent / summed).astype(jnp.bfloat16)
        attended = jnp.einsum(
            "hqk,khd->qhd", attn_probs, values_slot, preferred_element_type=jnp.float32
        )
        return (attended, (row_peak + jnp.log(summed))[..., 0])

    block_ids = jnp.arange(rows_all // block_rows, dtype=jnp.int32)
    attended, log_sums = lax.map(attention_one_block, block_ids)
    return (attended.reshape(rows_all, -1), log_sums)


def attention_backward(queries, keys, values, lengths, log_sums, grad_out, scale):
    rows_all = queries.shape[0]
    block_rows = min(512, SEQ_MAX)
    per_slot = SEQ_MAX // block_rows

    def one_slot(slot_index):
        keys_slot = lax.dynamic_slice_in_dim(keys, slot_index * SEQ_MAX, SEQ_MAX, 0)
        values_slot = lax.dynamic_slice_in_dim(values, slot_index * SEQ_MAX, SEQ_MAX, 0)
        length = lax.dynamic_index_in_dim(lengths, slot_index, 0, keepdims=False)

        def one_one_block(carried, block_index):
            grad_keys, grad_values = carried
            row_start = slot_index * SEQ_MAX + block_index * block_rows
            query_blk = lax.dynamic_slice_in_dim(queries, row_start, block_rows, 0)
            grad_blk = lax.dynamic_slice_in_dim(grad_out, row_start, block_rows, 0)
            lse_blk = lax.dynamic_index_in_dim(
                log_sums, slot_index * per_slot + block_index, 0, keepdims=False
            )
            scores = masked_scores(query_blk, keys_slot, length, scale)
            attn_probs = jnp.exp(scores - lse_blk[..., None])
            grad_values = grad_values + jnp.einsum(
                "hqk,qhd->khd",
                attn_probs.astype(jnp.bfloat16),
                grad_blk,
                preferred_element_type=jnp.float32,
            )
            grad_probs = jnp.einsum(
                "qhd,khd->hqk", grad_blk, values_slot, preferred_element_type=jnp.float32
            )
            inner = jnp.sum(attn_probs * grad_probs, axis=-1, keepdims=True)
            grad_scores = (attn_probs * (grad_probs - inner)).astype(jnp.bfloat16)
            grad_query = (
                jnp.einsum(
                    "hqk,khd->qhd", grad_scores, keys_slot, preferred_element_type=jnp.float32
                )
                * scale
            )
            grad_keys = (
                grad_keys
                + jnp.einsum(
                    "hqk,qhd->khd", grad_scores, query_blk, preferred_element_type=jnp.float32
                )
                * scale
            )
            return ((grad_keys, grad_values), grad_query)

        zero_slot = jnp.zeros(keys_slot.shape, jnp.float32)
        (grad_keys, grad_values), grad_queries = lax.scan(
            one_one_block, (zero_slot, zero_slot), jnp.arange(per_slot, dtype=jnp.int32)
        )
        return (grad_queries.reshape(keys_slot.shape), grad_keys, grad_values)

    slot_ids = jnp.arange(rows_all // SEQ_MAX, dtype=jnp.int32)
    grad_q, grad_k, grad_v = lax.map(one_slot, slot_ids)
    width = queries.shape[1] * queries.shape[2]
    return (
        grad_q.reshape(rows_all, width).astype(jnp.bfloat16),
        grad_k.reshape(rows_all, width).astype(jnp.bfloat16),
        grad_v.reshape(rows_all, width).astype(jnp.bfloat16),
    )


def per_device_split_heads(
    tokens,
    cotangent,
    seq_lengths,
    slot_seq,
    w_query,
    w_key,
    w_value,
    b_query,
    b_value,
    w_output,
    b_output,
    gain_first,
    shift_first,
    w_up,
    b_up,
    w_down,
    b_down,
    gain_second,
    shift_second,
):
    local_rows = tokens.shape[0]
    group_rows = local_rows * lax.axis_size("tensor")
    slot_count = group_rows // SEQ_MAX
    group_index = lax.axis_index("dp")
    my_slots = lax.dynamic_slice_in_dim(slot_seq, group_index * slot_count, slot_count, 0)
    seq_ids = jnp.arange(seq_lengths.shape[0], dtype=jnp.int32)
    lengths = jnp.sum(
        jnp.where(my_slots[:, None] == seq_ids[None, :], seq_lengths[None, :], 0), axis=1
    )
    scale = HEAD_DIM ** (-0.5)
    (
        query_full,
        key_full,
        value_full,
        bias_query,
        bias_value,
        out_rows,
        up_full,
        bias_up,
        down_full,
    ) = (
        lax.all_gather(w_query, "dp", axis=0, tiled=True),
        lax.all_gather(w_key, "dp", axis=0, tiled=True),
        lax.all_gather(w_value, "dp", axis=0, tiled=True),
        lax.all_gather(b_query, "dp", axis=1, tiled=True),
        lax.all_gather(b_value, "dp", axis=1, tiled=True),
        lax.all_gather(w_output, "dp", axis=1, tiled=True),
        lax.all_gather(w_up, "dp", axis=0, tiled=True),
        lax.all_gather(b_up, "dp", axis=1, tiled=True),
        lax.all_gather(w_down, "dp", axis=1, tiled=True),
    )
    bias_out, bias_down, gain_one, shift_one, gain_two, shift_two = (
        lax.all_gather(b_output, ("dp", "tensor"), axis=0, tiled=True),
        lax.all_gather(b_down, ("dp", "tensor"), axis=0, tiled=True),
        lax.all_gather(gain_first, ("dp", "tensor"), axis=0, tiled=True),
        lax.all_gather(shift_first, ("dp", "tensor"), axis=0, tiled=True),
        lax.all_gather(gain_second, ("dp", "tensor"), axis=0, tiled=True),
        lax.all_gather(shift_second, ("dp", "tensor"), axis=0, tiled=True),
    )
    tokens_all = lax.all_gather(tokens, "tensor", axis=0, tiled=True)
    queries = (matmul(tokens_all, query_full) + bias_query.reshape(-1).astype(jnp.float32)).astype(
        jnp.bfloat16
    )
    keys = matmul(tokens_all, key_full).astype(jnp.bfloat16)
    values = (matmul(tokens_all, value_full) + bias_value.reshape(-1).astype(jnp.float32)).astype(
        jnp.bfloat16
    )
    heads_local = queries.shape[1] // HEAD_DIM
    shape_three = (group_rows, heads_local, HEAD_DIM)
    queries_three = queries.reshape(shape_three)
    keys_three = keys.reshape(shape_three)
    values_three = values.reshape(shape_three)
    attended, log_sums = attention_forward(queries_three, keys_three, values_three, lengths, scale)
    mixed = attended.astype(jnp.bfloat16)
    branch = lax.psum_scatter(matmul(mixed, out_rows), "tensor", scatter_dimension=0, tiled=True)
    resid_one = tokens.astype(jnp.float32) + (branch + bias_out)
    normed, normal_one, inv_one = norm_forward(resid_one, gain_one, shift_one)
    normed_all = lax.all_gather(normed.astype(jnp.bfloat16), "tensor", axis=0, tiled=True)
    hidden_pre = matmul(normed_all, up_full) + bias_up.reshape(-1).astype(jnp.float32)
    hidden = jax.nn.gelu(hidden_pre, approximate=False).astype(jnp.bfloat16)
    second = lax.psum_scatter(
        matmul(hidden, down_full).astype(jnp.bfloat16), "tensor", scatter_dimension=0, tiled=True
    ).astype(jnp.float32)
    resid_two = normed + (second + bias_down)
    layer_out, normal_two, inv_two = norm_forward(resid_two, gain_two, shift_two)
    grad_two, grad_gain_two, grad_shift_two = norm_backward(
        normal_two, inv_two, gain_two, cotangent.astype(jnp.float32)
    )
    grad_second = grad_two.astype(jnp.bfloat16)
    grad_bias_down = jnp.sum(grad_second, axis=0, dtype=jnp.float32)
    grad_second_all = lax.all_gather(grad_second, "tensor", axis=0, tiled=True)
    grad_down = contract_rows(hidden, grad_second_all)
    grad_hidden = contract_cols(grad_second_all, down_full)
    gelu_value, gelu_pull = jax.vjp(
        lambda pre_act: jax.nn.gelu(pre_act, approximate=False), hidden_pre
    )
    grad_pre = gelu_pull(grad_hidden)[0].astype(jnp.bfloat16)
    grad_upw = contract_rows(normed_all, grad_pre)
    grad_bias_up = jnp.sum(grad_pre, axis=0, dtype=jnp.float32).reshape(-1, HEAD_DIM)
    grad_normed = grad_two + lax.psum_scatter(
        contract_cols(grad_pre, up_full), "tensor", scatter_dimension=0, tiled=True
    )
    grad_one, grad_gain_one, grad_shift_one = norm_backward(
        normal_one, inv_one, gain_one, grad_normed
    )
    grad_branch = grad_one.astype(jnp.bfloat16)
    grad_bias_out = jnp.sum(grad_branch, axis=0, dtype=jnp.float32)
    grad_branch_all = lax.all_gather(grad_branch, "tensor", axis=0, tiled=True)
    grad_outw = contract_rows(mixed, grad_branch_all)
    grad_mixed = contract_cols(grad_branch_all, out_rows).astype(jnp.bfloat16)
    grad_queries, grad_keys, grad_values = attention_backward(
        queries_three,
        keys_three,
        values_three,
        lengths,
        log_sums,
        grad_mixed.reshape(shape_three),
        scale,
    )
    grad_queryw = contract_rows(tokens_all, grad_queries)
    grad_keyw = contract_rows(tokens_all, grad_keys)
    grad_valuew = contract_rows(tokens_all, grad_values)
    grad_bias_query = jnp.sum(grad_queries, axis=0, dtype=jnp.float32).reshape(
        heads_local, HEAD_DIM
    )
    grad_bias_value = jnp.sum(grad_values, axis=0, dtype=jnp.float32).reshape(heads_local, HEAD_DIM)
    query_part = contract_cols(grad_queries, query_full)
    key_part = contract_cols(grad_keys, key_full)
    value_part = contract_cols(grad_values, value_full)
    grad_tokens = grad_one + lax.psum_scatter(
        (query_part + key_part + value_part).astype(jnp.bfloat16),
        "tensor",
        scatter_dimension=0,
        tiled=True,
    ).astype(jnp.float32)
    out_wq, out_wk, out_wv, out_bq, out_bv, out_wo, out_wup, out_bup, out_wdown = (
        lax.psum_scatter(
            grad_queryw.astype(jnp.bfloat16), "dp", scatter_dimension=0, tiled=True
        ).astype(jnp.float32),
        lax.psum_scatter(
            grad_keyw.astype(jnp.bfloat16), "dp", scatter_dimension=0, tiled=True
        ).astype(jnp.float32),
        lax.psum_scatter(
            grad_valuew.astype(jnp.bfloat16), "dp", scatter_dimension=0, tiled=True
        ).astype(jnp.float32),
        lax.psum_scatter(
            grad_bias_query.astype(jnp.bfloat16), "dp", scatter_dimension=1, tiled=True
        ).astype(jnp.float32),
        lax.psum_scatter(
            grad_bias_value.astype(jnp.bfloat16), "dp", scatter_dimension=1, tiled=True
        ).astype(jnp.float32),
        lax.psum_scatter(
            grad_outw.astype(jnp.bfloat16), "dp", scatter_dimension=1, tiled=True
        ).astype(jnp.float32),
        lax.psum_scatter(
            grad_upw.astype(jnp.bfloat16), "dp", scatter_dimension=0, tiled=True
        ).astype(jnp.float32),
        lax.psum_scatter(
            grad_bias_up.astype(jnp.bfloat16), "dp", scatter_dimension=1, tiled=True
        ).astype(jnp.float32),
        lax.psum_scatter(
            grad_down.astype(jnp.bfloat16), "dp", scatter_dimension=1, tiled=True
        ).astype(jnp.float32),
    )
    out_bo, out_bdown, out_gain_one, out_shift_one, out_gain_two, out_shift_two = (
        lax.psum_scatter(grad_bias_out, ("dp", "tensor"), scatter_dimension=0, tiled=True),
        lax.psum_scatter(grad_bias_down, ("dp", "tensor"), scatter_dimension=0, tiled=True),
        lax.psum_scatter(grad_gain_one, ("dp", "tensor"), scatter_dimension=0, tiled=True),
        lax.psum_scatter(grad_shift_one, ("dp", "tensor"), scatter_dimension=0, tiled=True),
        lax.psum_scatter(grad_gain_two, ("dp", "tensor"), scatter_dimension=0, tiled=True),
        lax.psum_scatter(grad_shift_two, ("dp", "tensor"), scatter_dimension=0, tiled=True),
    )
    return (
        layer_out,
        grad_tokens,
        out_wq,
        out_wk,
        out_wv,
        out_bq,
        out_bv,
        out_wo,
        out_bo,
        out_gain_one,
        out_shift_one,
        out_wup,
        out_bup,
        out_wdown,
        out_bdown,
        out_gain_two,
        out_shift_two,
    )


PAIR = 2 * HEAD_DIM
QUERY_ROWS = 512
KEY_ROWS = 512
LAST_DIMS = (((1,), (1,)), ((), ()))
FIRST_DIMS = (((0,), (0,)), ((), ()))


def dot32(left, right, dims):
    return lax.dot_general(left, right, dims, preferred_element_type=jnp.float32)


def lanes_of(rows):
    return lax.broadcasted_iota(jnp.int32, (rows, PAIR), 1)


def head_mask(rows, head):
    first = (lanes_of(rows) < HEAD_DIM).astype(jnp.float32)
    return first if head == 0 else 1.0 - first


def three_parts(column, rows, lead):
    high = column.astype(jnp.bfloat16).astype(jnp.float32)
    rest = column - high
    middle = rest.astype(jnp.bfloat16).astype(jnp.float32)
    low = rest - middle
    lane = lanes_of(rows)
    out = jnp.where(lane == 0, lead, 0.0)
    out = jnp.where(lane == 1, high, out)
    out = jnp.where(lane == 2, middle, out)
    return jnp.where(lane == 3, low, out).astype(jnp.bfloat16)


def forward_kernel(q_ref, k_ref, v_ref, extra_ref, out_ref, lse_ref):
    rows = q_ref.shape[0]
    query_blk = q_ref[...] * jnp.bfloat16(HEAD_DIM**-0.5)
    keys_wide = jnp.concatenate([k_ref[...], extra_ref[...]], axis=1)
    one_lane = (lanes_of(rows) == 0).astype(jnp.float32).astype(jnp.bfloat16)
    results = []
    for head in range(2):
        mask = head_mask(rows, head).astype(jnp.bfloat16)
        query_wide = jnp.concatenate([query_blk * mask, one_lane], axis=1)
        scores = dot32(query_wide, keys_wide, LAST_DIMS)
        peak = jnp.max(scores, axis=-1, keepdims=True)
        exponent = jnp.exp(scores - peak).astype(jnp.bfloat16)
        own = head_mask(SEQ_MAX, head)
        values_ones = v_ref[...] * own.astype(jnp.bfloat16) + (1.0 - own).astype(jnp.bfloat16)
        mixed = jnp.dot(exponent, values_ones, preferred_element_type=jnp.float32)
        summed = pltpu.roll(mixed, HEAD_DIM, 1)
        results.append((mixed / summed, peak + jnp.log(summed)))
    first = lanes_of(rows) < HEAD_DIM
    out_ref[...] = jnp.where(first, results[0][0], results[1][0]).astype(jnp.bfloat16)
    lse_ref[...] = jnp.where(first, results[0][1], results[1][1])


def backward_kernel(
    q_ref, k_ref, v_ref, extra_ref, grad_ref, out_ref, lse_ref, dq_ref, dk_ref, dv_ref, dk_acc, dv_acc
):
    rows = q_ref.shape[0]

    @pl.when(pl.program_id(2) == 0)
    def _():
        dk_acc[...] = jnp.zeros_like(dk_acc)
        dv_acc[...] = jnp.zeros_like(dv_acc)

    query_blk = q_ref[...] * jnp.bfloat16(HEAD_DIM**-0.5)
    product = grad_ref[...].astype(jnp.float32) * out_ref[...].astype(jnp.float32)
    heads = []
    for head in range(2):
        mask = head_mask(rows, head)
        mask_low = mask.astype(jnp.bfloat16)
        inner = jnp.sum(product * mask, axis=-1, keepdims=True)
        lse = lse_ref[:, head * HEAD_DIM : head * HEAD_DIM + 1]
        query_own = query_blk * mask_low
        grad_own = grad_ref[...] * mask_low
        query_wide = jnp.concatenate([query_own, three_parts(-lse, rows, 1.0)], axis=1)
        grad_wide = jnp.concatenate([grad_own, three_parts(-inner, rows, 0.0)], axis=1)
        heads.append((query_own, grad_own, query_wide, grad_wide))
    grad_query = jnp.zeros((PAIR, rows), jnp.float32)
    for chunk in range(SEQ_MAX // KEY_ROWS):
        span = pl.ds(chunk * KEY_ROWS, KEY_ROWS)
        keys_blk = k_ref[span, :]
        keys_wide = jnp.concatenate([keys_blk, extra_ref[span, :]], axis=1)
        values_wide = jnp.concatenate([v_ref[span, :], extra_ref[span, :]], axis=1)
        dk_sum = dk_acc[span, :]
        dv_sum = dv_acc[span, :]
        for head in range(2):
            query_own, grad_own, query_wide, grad_wide = heads[head]
            probs = jnp.exp(dot32(keys_wide, query_wide, LAST_DIMS))
            grad_probs = dot32(values_wide, grad_wide, LAST_DIMS)
            grad_scores = (probs * grad_probs).astype(jnp.bfloat16)
            dv_sum = dv_sum + jnp.dot(
                probs.astype(jnp.bfloat16), grad_own, preferred_element_type=jnp.float32
            )
            dk_sum = dk_sum + jnp.dot(grad_scores, query_own, preferred_element_type=jnp.float32)
            keys_own = keys_blk * head_mask(KEY_ROWS, head).astype(jnp.bfloat16)
            grad_query = grad_query + dot32(keys_own, grad_scores, FIRST_DIMS)
        dk_acc[span, :] = dk_sum
        dv_acc[span, :] = dv_sum
    dq_ref[...] = (grad_query.T * HEAD_DIM**-0.5).astype(jnp.bfloat16)

    @pl.when(pl.program_id(2) == pl.num_programs(2) - 1)
    def _():
        dk_ref[...] = dk_acc[...].astype(jnp.bfloat16)
        dv_ref[...] = dv_acc[...].astype(jnp.bfloat16)


def attention_specs(width):
    pairs = width // PAIR
    steps = SEQ_MAX // QUERY_ROWS

    def row_spec(offset):
        return pl.BlockSpec((QUERY_ROWS, PAIR), lambda s, p, i: (s * steps + i, p + offset * pairs))

    def slot_spec(offset):
        return pl.BlockSpec((SEQ_MAX, PAIR), lambda s, p, i: (s, p + offset * pairs))

    extra_spec = pl.BlockSpec((SEQ_MAX, PAIR), lambda s, p, i: (s, 0))
    return pairs, steps, row_spec, slot_spec, extra_spec


def attention_call(qkv, extra):
    rows, width = qkv.shape[0], qkv.shape[1] // 3
    pairs, steps, row_spec, slot_spec, extra_spec = attention_specs(width)
    return pl.pallas_call(
        forward_kernel,
        grid=(rows // SEQ_MAX, pairs, steps),
        in_specs=[row_spec(0), slot_spec(1), slot_spec(2), extra_spec],
        out_specs=[row_spec(0), row_spec(0)],
        out_shape=[
            jax.ShapeDtypeStruct((rows, width), jnp.bfloat16),
            jax.ShapeDtypeStruct((rows, width), jnp.float32),
        ],
        compiler_params=pltpu.CompilerParams(vmem_limit_bytes=48 * 2**20),
        cost_estimate=pl.CostEstimate(
            flops=16 * rows * SEQ_MAX * width,
            bytes_accessed=14 * rows * width,
            transcendentals=rows * SEQ_MAX * width // HEAD_DIM,
        ),
    )(qkv, qkv, qkv, extra)


def attention_pull(qkv, extra, grad_mixed, mixed, log_sums):
    rows, width = mixed.shape
    pairs, steps, row_spec, slot_spec, extra_spec = attention_specs(width)
    shape = jax.ShapeDtypeStruct((rows, width), jnp.bfloat16)
    return pl.pallas_call(
        backward_kernel,
        grid=(rows // SEQ_MAX, pairs, steps),
        in_specs=[row_spec(0), slot_spec(1), slot_spec(2), extra_spec]
        + [row_spec(0), row_spec(0), row_spec(0)],
        out_specs=[row_spec(0), slot_spec(0), slot_spec(0)],
        out_shape=[shape, shape, shape],
        scratch_shapes=[pltpu.VMEM((SEQ_MAX, PAIR), jnp.float32)] * 2,
        compiler_params=pltpu.CompilerParams(vmem_limit_bytes=48 * 2**20),
        cost_estimate=pl.CostEstimate(
            flops=40 * rows * SEQ_MAX * width,
            bytes_accessed=20 * rows * width,
            transcendentals=rows * SEQ_MAX * width // HEAD_DIM,
        ),
    )(qkv, qkv, qkv, extra, grad_mixed, mixed, log_sums)


def gelu_both(pre_act):
    size = jnp.abs(pre_act)
    bell = jnp.exp(-0.5 * pre_act * pre_act)
    t = 1.0 / (1.0 + (0.3275911 * 0.5**0.5) * size)
    poly = 1.061405429
    for coefficient in (-1.453152027, 1.421413741, -0.284496736, 0.254829592):
        poly = poly * t + coefficient
    tail = 0.5 * poly * t * bell
    cdf = jnp.where(pre_act >= 0, 1.0 - tail, tail)
    return (pre_act * cdf, cdf + pre_act * bell * 0.3989422804014327)


def both_halves(gathered, start, size):
    return jnp.concatenate(
        [gathered[i, :, start : start + size] for i in range(gathered.shape[0])], axis=1
    )


def split_halves(whole, parts):
    shard, width = whole.shape
    return whole.reshape(shard, parts, width // parts)


def per_device(
    tokens,
    cotangent,
    seq_lengths,
    slot_seq,
    w_query,
    w_key,
    w_value,
    b_query,
    b_value,
    w_output,
    b_output,
    gain_first,
    shift_first,
    w_up,
    b_up,
    w_down,
    b_down,
    gain_second,
    shift_second,
):
    local_rows, width = tokens.shape
    n_dp, n_tensor = lax.axis_size("dp"), lax.axis_size("tensor")
    both = ("dp", "tensor")
    slots = local_rows // SEQ_MAX
    my_index = lax.axis_index("dp") * n_tensor + lax.axis_index("tensor")
    my_slots = lax.dynamic_slice_in_dim(slot_seq, my_index * slots, slots, 0)
    seq_ids = jnp.arange(seq_lengths.shape[0], dtype=jnp.int32)
    lengths = jnp.sum(
        jnp.where(my_slots[:, None] == seq_ids[None, :], seq_lengths[None, :], 0), axis=1
    )
    valid = jnp.arange(SEQ_MAX, dtype=jnp.int32)[None, :] < lengths[:, None]
    key_bias = jnp.where(valid, 0.0, masked_score).reshape(-1, 1)
    lane = jnp.arange(PAIR, dtype=jnp.int32)[None, :]
    extra = jnp.where(
        lane == 0, key_bias, jnp.where((lane >= 1) & (lane <= 3), 1.0, 0.0)
    ).astype(jnp.bfloat16)

    pieces = (w_query, w_key, w_value, w_output.T, w_up, w_down.T)
    halves = lax.all_gather(jnp.concatenate(pieces, axis=1), "tensor", axis=0)
    shards, start = [], 0
    for piece in pieces:
        shards.append(both_halves(halves, start, piece.shape[1]))
        start += piece.shape[1]
    qkv_full = lax.all_gather(jnp.concatenate(shards[:3], axis=1), "dp", axis=0, tiled=True)
    out_t = lax.all_gather(shards[3], "dp", axis=0, tiled=True)
    up_full = lax.all_gather(shards[4], "dp", axis=0, tiled=True)
    down_t = lax.all_gather(shards[5], "dp", axis=0, tiled=True)

    vectors = (b_output, b_down, gain_first, shift_first, gain_second, shift_second)
    biases = (b_query, b_value, b_up)
    small = jnp.concatenate(
        list(vectors) + [bias.reshape(-1).astype(jnp.float32) for bias in biases]
    )
    small_all = lax.all_gather(small, both, axis=0)
    each = b_output.shape[0]
    bias_out, bias_down, gain_one, shift_one, gain_two, shift_two = [
        small_all[:, i * each : (i + 1) * each].reshape(-1) for i in range(len(vectors))
    ]
    start, whole_biases = len(vectors) * each, []
    for bias in biases:
        block = small_all[:, start : start + bias.size]
        block = block.reshape((n_dp, n_tensor) + bias.shape).transpose(1, 2, 0, 3)
        whole_biases.append(block.reshape(-1))
        start += bias.size
    bias_query, bias_value, bias_up = whole_biases
    bias_qkv = jnp.concatenate([bias_query, jnp.zeros_like(bias_query), bias_value])

    qkv = (matmul(tokens, qkv_full) + bias_qkv).astype(jnp.bfloat16)
    mixed, log_sums = attention_call(qkv, extra)
    resid_one = tokens.astype(jnp.float32) + (contract_cols(mixed, out_t) + bias_out)
    normed, normal_one, inv_one = norm_forward(resid_one, gain_one, shift_one)
    normed_low = normed.astype(jnp.bfloat16)
    hidden, slope = gelu_both(matmul(normed_low, up_full) + bias_up)
    hidden, slope = hidden.astype(jnp.bfloat16), slope.astype(jnp.bfloat16)
    resid_two = normed + (contract_cols(hidden, down_t) + bias_down)
    layer_out, normal_two, inv_two = norm_forward(resid_two, gain_two, shift_two)
    grad_two, grad_gain_two, grad_shift_two = norm_backward(
        normal_two, inv_two, gain_two, cotangent.astype(jnp.float32)
    )
    grad_second = grad_two.astype(jnp.bfloat16)
    grad_bias_down = jnp.sum(grad_second, axis=0, dtype=jnp.float32)

    def reduce_dp(grad):
        return lax.psum_scatter(grad.astype(jnp.bfloat16), "dp", scatter_dimension=0, tiled=True)

    sum_down = reduce_dp(contract_rows(grad_second, hidden))
    grad_pre = (matmul(grad_second, down_t) * slope.astype(jnp.float32)).astype(jnp.bfloat16)
    sum_up = reduce_dp(contract_rows(normed_low, grad_pre))
    grad_bias_up = jnp.sum(grad_pre, axis=0, dtype=jnp.float32)
    grad_normed = grad_two + contract_cols(grad_pre, up_full)
    grad_one, grad_gain_one, grad_shift_one = norm_backward(
        normal_one, inv_one, gain_one, grad_normed
    )
    grad_branch = grad_one.astype(jnp.bfloat16)
    grad_bias_out = jnp.sum(grad_branch, axis=0, dtype=jnp.float32)
    sum_out = reduce_dp(contract_rows(grad_branch, mixed))
    grad_mixed = matmul(grad_branch, out_t).astype(jnp.bfloat16)
    grad_queries, grad_keys, grad_values = attention_pull(qkv, extra, grad_mixed, mixed, log_sums)
    grad_qkv = jnp.concatenate([grad_queries, grad_keys, grad_values], axis=1)
    sum_qkv = reduce_dp(contract_rows(tokens, grad_qkv))
    grad_bias_query = jnp.sum(grad_queries, axis=0, dtype=jnp.float32)
    grad_bias_value = jnp.sum(grad_values, axis=0, dtype=jnp.float32)
    grad_tokens = grad_one + contract_cols(grad_qkv, qkv_full)

    sums = [sum_qkv[:, i * width : (i + 1) * width] for i in range(3)] + [sum_out, sum_up, sum_down]
    packed = jnp.concatenate([split_halves(total, n_tensor) for total in sums], axis=2)
    packed = lax.psum_scatter(packed, "tensor", scatter_dimension=1, tiled=False)
    packed = packed.astype(jnp.float32)
    owned, start = [], 0
    for piece in pieces:
        owned.append(packed[:, start : start + piece.shape[1]])
        start += piece.shape[1]
    out_wq, out_wk, out_wv, out_wo, out_wup, out_wdown = owned

    grad_vectors = (
        grad_bias_out,
        grad_bias_down,
        grad_gain_one,
        grad_shift_one,
        grad_gain_two,
        grad_shift_two,
    )
    columns = [vector.reshape(n_dp * n_tensor, each) for vector in grad_vectors]
    for bias, grad in zip(biases, (grad_bias_query, grad_bias_value, grad_bias_up)):
        block = grad.reshape(n_tensor, bias.shape[0], n_dp, bias.shape[1]).transpose(2, 0, 1, 3)
        columns.append(block.reshape(n_dp * n_tensor, bias.size))
    small_sum = lax.psum_scatter(
        jnp.concatenate(columns, axis=1), both, scatter_dimension=0, tiled=False
    )
    out_bo, out_bdown, out_gain_one, out_shift_one, out_gain_two, out_shift_two = [
        small_sum[i * each : (i + 1) * each] for i in range(len(grad_vectors))
    ]
    start, out_biases = len(grad_vectors) * each, []
    for bias in biases:
        out_biases.append(small_sum[start : start + bias.size].reshape(bias.shape))
        start += bias.size
    out_bq, out_bv, out_bup = out_biases
    return (
        layer_out,
        grad_tokens,
        out_wq,
        out_wk,
        out_wv,
        out_bq,
        out_bv,
        out_wo.T,
        out_bo,
        out_gain_one,
        out_shift_one,
        out_wup,
        out_bup,
        out_wdown.T,
        out_bdown,
        out_gain_two,
        out_shift_two,
    )


def choose_plan(*args):
    plan = per_device if args[0].shape[0] % SEQ_MAX == 0 else per_device_split_heads
    return plan(*args)


def solution(mesh):
    in_specs = (
        P(("dp", "tensor"), None),
        P(("dp", "tensor"), None),
        P(),
        P(),
        P("dp", "tensor"),
        P("dp", "tensor"),
        P("dp", "tensor"),
        P("tensor", "dp"),
        P("tensor", "dp"),
        P("tensor", "dp"),
        P(("dp", "tensor")),
        P(("dp", "tensor")),
        P(("dp", "tensor")),
        P("dp", "tensor"),
        P("tensor", "dp"),
        P("tensor", "dp"),
        P(("dp", "tensor")),
        P(("dp", "tensor")),
        P(("dp", "tensor")),
    )
    out_specs = (
        P(("dp", "tensor"), None),
        P(("dp", "tensor"), None),
        P("dp", "tensor"),
        P("dp", "tensor"),
        P("dp", "tensor"),
        P("tensor", "dp"),
        P("tensor", "dp"),
        P("tensor", "dp"),
        P(("dp", "tensor")),
        P(("dp", "tensor")),
        P(("dp", "tensor")),
        P("dp", "tensor"),
        P("tensor", "dp"),
        P("tensor", "dp"),
        P(("dp", "tensor")),
        P(("dp", "tensor")),
        P(("dp", "tensor")),
    )
    return jax.shard_map(
        choose_plan, mesh=mesh, in_specs=in_specs, out_specs=out_specs, check_vma=False
    )
```
